32 devices in a mesh: seq: 16 (over z, y, core), head: 2 (over x).
Axes of the slice: x: 2, y: 2, z: 4, core: 2. Of those that a mesh axis runs over, the one named last changes fastest.
Arguments:
- query_tensor: float32 [8192, 32, 128], P('seq', 'head'), may hold values from -6 to 6
- key_tensor: float32 [8192, 16, 128], P('seq', 'head'), may hold values from -6 to 6
- value_tensor: float32 [8192, 16, 128], P('seq', 'head'), may hold values from -6 to 6
- output_gradient: float32 [8192, 32, 128], P('seq', 'head'), may hold values from -24 to 24
- logsumexp: float32 [32, 8192], P('head', 'seq'), may hold values from 5.5 to 7
- row_inner_products: float32 [32, 8192], P('head', 'seq'), may hold values from -120 to 120
Outputs:
- query_grad: float32 [8192, 32, 128], P('seq', 'head')
- key_grad: float32 [8192, 16, 128], P('seq', 'head')
- value_grad: float32 [8192, 16, 128], P('seq', 'head')
The draws below stay inside these ranges and needn't reach their ends.
All inputs are finite; a program needn't handle non-finite values.
Results may differ from the reference program's by a relative error of at most 0.0053.
Values may be sent and summed in bfloat16 or wider, within the bound.
A program may use at most 192 MiB of HBM per device.

```python
import jax
import jax.numpy as jnp
from jax import lax

QUERY_HEADS = 32
KEY_VALUE_HEADS = 16
HEAD_SIZE = 128
WINDOW = 1024
QSCALE = 168
TOK_DEV = 512
SEQUENCE_TOKENS = 8192


def block_scale(own_key, dims, pieces, low, high):
    def one(dim, shards_of):
        steps = jax.random.uniform(jax.random.fold_in(jax.random.fold_in(own_key, 6), dim), (shards_of,), jnp.float32, low / len(pieces), high / len(pieces))
        return jnp.repeat(jnp.exp(steps), dims[dim] // shards_of).reshape((-1,) + (1,) * (len(dims) - dim - 1))

    loudness = one(*pieces[0])
    for cut in pieces[1:]:
        loudness = loudness * one(*cut)
    return loudness


def normal_values(rng, extent, scale, most, pieces=(), held_as=jnp.bfloat16):
    gain = block_scale(rng, extent, pieces, -0.22, 0.18) if pieces else 1.0
    array = jax.random.normal(rng, extent, jnp.float32) * scale * gain
    return jnp.minimum(jnp.maximum(array, -most), most).astype(held_as)


def setup_inputs(seed: int = 0) -> dict:
    splits = jax.random.split(jax.random.key(seed), 7)
    query_tensor = normal_values(splits[0], (SEQUENCE_TOKENS, QUERY_HEADS, HEAD_SIZE), 1.0, 6.0, ((0, 16), (1, 2)), jnp.float32)
    key_tensor = normal_values(splits[1], (SEQUENCE_TOKENS, KEY_VALUE_HEADS, HEAD_SIZE), 1.0, 6.0, ((0, 16), (1, 2)), jnp.float32)
    value_tensor = normal_values(splits[2], (SEQUENCE_TOKENS, KEY_VALUE_HEADS, HEAD_SIZE), 1.0, 6.0, ((0, 16), (1, 2)), jnp.float32)
    output_gradient = normal_values(splits[3], (SEQUENCE_TOKENS, QUERY_HEADS, HEAD_SIZE), 4.0, 24.0, ((0, 16), (1, 2)), jnp.float32)
    logsumexp = jnp.clip(5.5 + 1.5 * jax.random.uniform(splits[4], (QUERY_HEADS, SEQUENCE_TOKENS), jnp.float32) ** block_scale(splits[4], (QUERY_HEADS, SEQUENCE_TOKENS), ((0, 2), (1, 16)), -0.2, 0.2), 5.5, 7.0)
    row_inner_products = normal_values(splits[5], (QUERY_HEADS, SEQUENCE_TOKENS), 20.0, 120.0, ((0, 2), (1, 16)), jnp.float32)
    return dict(query_tensor=query_tensor, key_tensor=key_tensor, value_tensor=value_tensor, output_gradient=output_gradient, logsumexp=logsumexp, row_inner_products=row_inner_products)


def block_terms(query_rows, gradient_list, lse_rows, output_dots, keys, values, allowed):
    scale = QSCALE ** -0.5
    scores = jnp.einsum('tkgd,skd->kgts', query_rows.astype(jnp.float32), keys.astype(jnp.float32))
    probs = jnp.where(allowed, jnp.exp(scale * scores - lse_rows[..., None]), 0.0)
    dprob = jnp.einsum('tkgd,skd->kgts', gradient_list.astype(jnp.float32), values.astype(jnp.float32))
    dscore = probs * (dprob - output_dots[..., None])
    probs_low = probs.astype(jnp.bfloat16).astype(jnp.float32)
    dscore_low = dscore.astype(jnp.bfloat16).astype(jnp.float32)
    dvalue = jnp.einsum('kgts,tkgd->skd', probs_low, gradient_list.astype(jnp.float32))
    dkey = scale * jnp.einsum('kgts,tkgd->skd', dscore_low, query_rows.astype(jnp.float32))
    dquery = scale * jnp.einsum('kgts,skd->tkgd', dscore_low, keys.astype(jnp.float32))
    return dquery, dkey, dvalue


def reference(query_tensor, key_tensor, value_tensor, output_gradient, logsumexp, row_inner_products):
    window_length = TOK_DEV
    blocks = SEQUENCE_TOKENS // window_length
    query_group = QUERY_HEADS // KEY_VALUE_HEADS
    query_rows = query_tensor.astype(jnp.bfloat16).reshape(SEQUENCE_TOKENS, KEY_VALUE_HEADS, query_group, HEAD_SIZE)
    gradient_list = output_gradient.astype(jnp.bfloat16).reshape(SEQUENCE_TOKENS, KEY_VALUE_HEADS, query_group, HEAD_SIZE)
    front_edge = jnp.zeros((2 * window_length, KEY_VALUE_HEADS, HEAD_SIZE), jnp.bfloat16)
    keys = jnp.concatenate([front_edge, key_tensor.astype(jnp.bfloat16)], 0)
    values = jnp.concatenate([front_edge, value_tensor.astype(jnp.bfloat16)], 0)
    log_sum_exponent = logsumexp.reshape(KEY_VALUE_HEADS, query_group, SEQUENCE_TOKENS)
    output_dots = row_inner_products.reshape(KEY_VALUE_HEADS, query_group, SEQUENCE_TOKENS)

    def advance(carry, index):
        dkey_all, dvalue_all = carry
        start = (index * window_length).astype(jnp.int32)
        query_block = lax.dynamic_slice_in_dim(query_rows, start, window_length, 0)
        grad_block = lax.dynamic_slice_in_dim(gradient_list, start, window_length, 0)
        lse_block = lax.dynamic_slice_in_dim(log_sum_exponent, start, window_length, 2)
        dots_block = lax.dynamic_slice_in_dim(output_dots, start, window_length, 2)
        key_block = lax.dynamic_slice_in_dim(keys, start, 3 * window_length, 0)
        value_block = lax.dynamic_slice_in_dim(values, start, 3 * window_length, 0)
        qpos = start + lax.broadcasted_iota(jnp.int32, (window_length, 3 * window_length), 0)
        kpos = start - 2 * window_length + lax.broadcasted_iota(jnp.int32, (window_length, 3 * window_length), 1)
        spread = qpos - kpos
        allowed = (spread >= 0) & (spread < WINDOW) & (kpos >= 0)
        dquery, dkey, dvalue = block_terms(query_block, grad_block, lse_block, dots_block, key_block, value_block, allowed)
        dkey_all = lax.dynamic_update_slice_in_dim(dkey_all, lax.dynamic_slice_in_dim(dkey_all, start, 3 * window_length, 0) + dkey, start, 0)
        dvalue_all = lax.dynamic_update_slice_in_dim(dvalue_all, lax.dynamic_slice_in_dim(dvalue_all, start, 3 * window_length, 0) + dvalue, start, 0)
        return (dkey_all, dvalue_all), dquery

    empty_buffer = jnp.zeros((SEQUENCE_TOKENS + 2 * window_length, KEY_VALUE_HEADS, HEAD_SIZE), jnp.float32)
    (dkey_all, dvalue_all), dqueries = lax.scan(advance, (empty_buffer, empty_buffer), jnp.arange(blocks, dtype=jnp.int32))
    return dqueries.reshape(SEQUENCE_TOKENS, QUERY_HEADS, HEAD_SIZE), dkey_all[2 * window_length:], dvalue_all[2 * window_length:]
```

```python
import functools
import math

import jax
import jax.numpy as jnp
from jax import lax
from jax.experimental import pallas as pl
from jax.experimental.pallas import tpu as pltpu
from jax.sharding import PartitionSpec as P

WINDOW = 1024
QSCALE = 168
SCALE = QSCALE ** (-0.5)
LOG2E = math.log2(math.e)
MESH = pl.DeviceIdType.MESH
BF16 = jnp.bfloat16
F32 = jnp.float32


def dot(a, b, ca, cb):
    return lax.dot_general(a, b, (((ca,), (cb,)), ((), ())), preferred_element_type=F32)


def kernel(
    tokens, kheads, group, devices,
    q_hbm, k_hbm, v_hbm, g_hbm, lse_ref, dots_ref,
    dq_hbm, dk_ref, dv_ref,
    q_ref, k_ref, v_ref, g_ref, dq_ref,
    own, far, near, gnear_out, gnear_in, gfar_out, gfar_in,
    held, dq_acc, qb, gb,
    load_sem, store_sem,
    far_send, far_recv, near_send, near_recv,
    gnear_send, gnear_recv, gfar_send, gfar_recv,
):
    qheads = kheads * group
    half = tokens // 2
    me = lax.axis_index("seq")
    core = lax.rem(me, 2)
    partner = me + 1 - 2 * core
    has_far = me >= 2
    has_near = me >= 1
    has_next = me + 2 < devices
    gets_near = jnp.logical_or(core == 0, has_far)

    loads = [
        pltpu.make_async_copy(src, dst, load_sem.at[n])
        for n, (src, dst) in enumerate(
            ((k_hbm, k_ref), (v_hbm, v_ref), (q_hbm, q_ref), (g_hbm, g_ref))
        )
    ]
    for load in loads:
        load.start()

    barrier = pltpu.get_barrier_semaphore()
    pl.semaphore_signal(barrier, inc=1, device_id={"seq": partner}, device_id_type=MESH)

    @pl.when(has_far)
    def _():
        pl.semaphore_signal(barrier, inc=1, device_id={"seq": me - 2}, device_id_type=MESH)

    @pl.when(has_next)
    def _():
        pl.semaphore_signal(barrier, inc=1, device_id={"seq": me + 2}, device_id_type=MESH)

    pl.semaphore_wait(barrier, 1 + has_far.astype(jnp.int32) + has_next.astype(jnp.int32))

    def remote(src, dst, send, recv, h, to):
        return pltpu.make_async_remote_copy(
            src_ref=src.at[h], dst_ref=dst.at[h], send_sem=send.at[h], recv_sem=recv.at[h],
            device_id={"seq": to}, device_id_type=MESH,
        )

    def far_copy(h):
        return remote(own, far, far_send, far_recv, h, me + 2)

    def near_own(h):
        return remote(own, near, near_send, near_recv, h, partner)

    def near_relay(h):
        return remote(far, near, near_send, near_recv, h, partner)

    def gnear_copy(h):
        return remote(gnear_out, gnear_in, gnear_send, gnear_recv, h, partner)

    def gfar_copy(h):
        return remote(gfar_out, gfar_in, gfar_send, gfar_recv, h, me - 2)

    loads[0].wait()
    loads[1].wait()

    def send_own(h, _):
        own[h, 0:tokens] = k_ref[pl.ds(h, tokens, stride=kheads), :].astype(BF16)
        own[h, tokens:] = v_ref[pl.ds(h, tokens, stride=kheads), :].astype(BF16)

        @pl.when(has_next)
        def _():
            far_copy(h).start()

        @pl.when(core == 0)
        def _():
            near_own(h).start()

        return 0

    lax.fori_loop(0, kheads, send_own, 0)
    loads[2].wait()
    loads[3].wait()

    def block(kind, h, kv, emit):
        for jb in range(2):
            k = kv[h, jb * half:(jb + 1) * half]
            v = kv[h, tokens + jb * half:tokens + (jb + 1) * half]
            dk = dv = None
            for g in range(group):
                lo, hi = 0, tokens
                if kind == "own":
                    lo = jb * half
                elif kind == "far":
                    hi = (jb + 1) * half
                rows = slice(g * tokens + lo, g * tokens + hi)
                q = qb[rows]
                go = gb[rows]
                lse = lse_ref[pl.ds(h * group + g, 1), lo:hi]
                dots = dots_ref[pl.ds(h * group + g, 1), lo:hi]
                s = dot(k, q, 1, 1)
                p = jnp.exp2(s * (SCALE * LOG2E) - lse * LOG2E)
                if kind != "near":
                    kpos = lax.broadcasted_iota(jnp.int32, p.shape, 0) + jb * half
                    qpos = lax.broadcasted_iota(jnp.int32, p.shape, 1) + lo
                    keep = qpos >= kpos if kind == "own" else qpos < kpos
                    p = jnp.where(keep, p, 0.0)
                ds = (p * (dot(v, go, 1, 1) - dots)).astype(BF16)
                dv_term = dot(p.astype(BF16), go, 1, 0)
                dk_term = dot(ds, q, 1, 0)
                dv = dv_term if dv is None else dv + dv_term
                dk = dk_term if dk is None else dk + dk_term
                dq = dot(ds, k, 0, 0)
                if kind == "own" and jb == 0:
                    dq_acc[rows] = dq
                else:
                    dq_acc[rows] += dq
            emit(jb, dk * SCALE, dv)

    def send_sum(h):
        slot = lax.rem(h, 2)
        gnear_copy(h).wait_recv()
        gfar_out[h] = (held[slot] + gnear_in[h].astype(F32)).astype(BF16)
        gfar_copy(h).start()

    def step(h, _):
        @pl.when(jnp.logical_and(core == 1, has_far))
        def _():
            far_copy(h).wait_recv()
            near_relay(h).start()

        for g in range(group):
            rows = slice(g * tokens, (g + 1) * tokens)
            at = pl.ds(h * group + g, tokens, stride=qheads)
            qb[rows] = q_ref[at, :].astype(BF16)
            gb[rows] = g_ref[at, :].astype(BF16)

        def emit_own(jb, dk, dv):
            at = pl.ds(jb * half * kheads + h, half, stride=kheads)
            dk_ref[at, :] = dk
            dv_ref[at, :] = dv

        block("own", h, own, emit_own)

        @pl.when(has_near)
        def _():
            jax.lax.cond(
                core == 0,
                lambda: near_relay(h).wait_recv(),
                lambda: near_own(h).wait_recv(),
            )

            def emit_near(jb, dk, dv):
                gnear_out[h, jb * half:(jb + 1) * half] = dk.astype(BF16)
                gnear_out[h, tokens + jb * half:tokens + (jb + 1) * half] = dv.astype(BF16)

            block("near", h, near, emit_near)
            gnear_copy(h).start()

        @pl.when(has_far)
        def _():
            @pl.when(core == 0)
            def _():
                far_copy(h).wait_recv()

            slot = lax.rem(h, 2)

            @pl.when(jnp.logical_and(core == 1, h >= 1))
            def _():
                send_sum(h - 1)

            def emit_far(jb, dk, dv):
                held[slot, jb * half:(jb + 1) * half] = dk
                held[slot, tokens + jb * half:tokens + (jb + 1) * half] = dv

            block("far", h, far, emit_far)

            @pl.when(core == 0)
            def _():
                gfar_out[h] = held[slot].astype(BF16)
                gfar_copy(h).start()

        for g in range(group):
            at = pl.ds(h * group + g, tokens, stride=qheads)
            dq_ref[at, :] = dq_acc[g * tokens:(g + 1) * tokens] * SCALE
        return 0

    lax.fori_loop(0, kheads, step, 0)

    @pl.when(jnp.logical_and(core == 1, has_far))
    def _():
        send_sum(kheads - 1)

    store = pltpu.make_async_copy(dq_ref, dq_hbm, store_sem)
    store.start()

    def finish(h, _):
        at = pl.ds(h, tokens, stride=kheads)

        @pl.when(core == 0)
        def _():
            gnear_copy(h).wait_recv()
            dk_ref[at, :] += gnear_in[h, 0:tokens].astype(F32)
            dv_ref[at, :] += gnear_in[h, tokens:].astype(F32)

        @pl.when(has_next)
        def _():
            gfar_copy(h).wait_recv()
            dk_ref[at, :] += gfar_in[h, 0:tokens].astype(F32)
            dv_ref[at, :] += gfar_in[h, tokens:].astype(F32)

        return 0

    lax.fori_loop(0, kheads, finish, 0)

    def drain(h, _):
        @pl.when(has_next)
        def _():
            far_copy(h).wait_send()

        @pl.when(gets_near)
        def _():
            near_own(h).wait_send()

        @pl.when(has_near)
        def _():
            gnear_copy(h).wait_send()

        @pl.when(has_far)
        def _():
            gfar_copy(h).wait_send()

        return 0

    lax.fori_loop(0, kheads, drain, 0)
    store.wait()


def on_device(devices, query, key, value, gradient, logsumexp, dots):
    tokens, qheads, width = query.shape
    kheads = key.shape[1]
    group = qheads // kheads
    assert WINDOW == 2 * tokens
    flat_q = (tokens * qheads, width)
    flat_k = (tokens * kheads, width)
    message = pltpu.VMEM((kheads, 2 * tokens, width), BF16)
    anywhere = pl.BlockSpec(memory_space=pl.ANY)
    vmem = pl.BlockSpec(memory_space=pltpu.VMEM)
    sems = pltpu.SemaphoreType.DMA((kheads,))
    dq, dk, dv = pl.pallas_call(
        functools.partial(kernel, tokens, kheads, group, devices),
        out_shape=(
            jax.ShapeDtypeStruct(flat_q, F32),
            jax.ShapeDtypeStruct(flat_k, F32),
            jax.ShapeDtypeStruct(flat_k, F32),
        ),
        in_specs=[anywhere] * 4 + [vmem] * 2,
        out_specs=(anywhere, vmem, vmem),
        scratch_shapes=[
            pltpu.VMEM(flat_q, F32),
            pltpu.VMEM(flat_k, F32),
            pltpu.VMEM(flat_k, F32),
            pltpu.VMEM(flat_q, F32),
            pltpu.VMEM(flat_q, F32),
        ] + [message] * 7 + [
            pltpu.VMEM((2, 2 * tokens, width), F32),
            pltpu.VMEM((group * tokens, width), F32),
            pltpu.VMEM((group * tokens, width), BF16),
            pltpu.VMEM((group * tokens, width), BF16),
            pltpu.SemaphoreType.DMA((4,)),
            pltpu.SemaphoreType.DMA,
        ] + [sems] * 8,
        compiler_params=pltpu.CompilerParams(
            collective_id=0, has_side_effects=True, vmem_limit_bytes=58 * 2**20
        ),
        cost_estimate=pl.CostEstimate(
            flops=10 * qheads * tokens * WINDOW * width,
            bytes_accessed=(3 * qheads + 4 * kheads) * tokens * width * 4,
            transcendentals=qheads * tokens * WINDOW,
        ),
    )(
        query.reshape(flat_q), key.reshape(flat_k), value.reshape(flat_k),
        gradient.reshape(flat_q), logsumexp, dots,
    )
    return dq.reshape(query.shape), dk.reshape(key.shape), dv.reshape(value.shape)


def solution(mesh):
    return jax.shard_map(
        functools.partial(on_device, mesh.shape["seq"]),
        mesh=mesh,
        in_specs=(
            P("seq", "head", None),
            P("seq", "head", None),
            P("seq", "head", None),
            P("seq", "head", None),
            P("head", "seq"),
            P("head", "seq"),
        ),
        out_specs=(P("seq", "head", None), P("seq", "head", None), P("seq", "head", None)),
        check_vma=False,
    )
```

```python
import functools
import math

import jax
import jax.numpy as jnp
from jax import lax
from jax.experimental import pallas as pl
from jax.experimental.pallas import tpu as pltpu
from jax.sharding import PartitionSpec as P

WINDOW = 1024
QSCALE = 168
SCALE = QSCALE ** (-0.5)
LOG2E = math.log2(math.e)
MESH = pl.DeviceIdType.MESH
BF16 = jnp.bfloat16
F32 = jnp.float32


def dot(a, b, ca, cb):
    return lax.dot_general(a, b, (((ca,), (cb,)), ((), ())), preferred_element_type=F32)


def kernel(
    tokens, kheads, group, devices,
    q_hbm, k_hbm, v_hbm, g_hbm, lse_ref, dots_ref,
    dq_hbm, dk_ref, dv_ref,
    q_ref, k_ref, v_ref, g_ref, dq_ref,
    own, far, near, relay, gnear_out, gnear_in, gfar_out, gfar_in,
    held, dq_acc, qb, gb,
    load_sem, store_sem,
    far_send, far_recv, near_send, near_recv,
    gnear_send, gnear_recv, gfar_send, gfar_recv, relay_send, relay_recv,
):
    qheads = kheads * group
    half = tokens // 2
    me = lax.axis_index("seq")
    core = lax.rem(me, 2)
    partner = me + 1 - 2 * core
    has_far = me >= 2
    has_near = me >= 1
    has_next = me + 2 < devices
    gets_near = jnp.logical_or(core == 0, has_far)
    pairs = devices // 4
    pair = me // 4
    odd = lax.rem(me // 2, 2) == 1

    def picked(h, share):
        return lax.rem(h * share, pairs) < share

    def both(*terms):
        return functools.reduce(jnp.logical_and, terms)

    def detours_forward(h):
        return both(odd, has_next, picked(h + 3, pair + 1))

    def relays_forward(h):
        return both(odd, pair >= 1, picked(h + 3, pair))

    def detours_back(h):
        return both(jnp.logical_not(odd), pair >= 1, picked(h, pairs - pair))

    def relays_back(h):
        return both(jnp.logical_not(odd), pair + 1 < pairs, picked(h, pairs - pair - 1))

    loads = [
        pltpu.make_async_copy(src, dst, load_sem.at[n])
        for n, (src, dst) in enumerate(
            ((k_hbm, k_ref), (v_hbm, v_ref), (q_hbm, q_ref), (g_hbm, g_ref))
        )
    ]
    loads[0].start()
    loads[1].start()

    barrier = pltpu.get_barrier_semaphore()
    pl.semaphore_signal(barrier, inc=1, device_id={"seq": partner}, device_id_type=MESH)

    @pl.when(has_far)
    def _():
        pl.semaphore_signal(barrier, inc=1, device_id={"seq": me - 2}, device_id_type=MESH)

    @pl.when(has_next)
    def _():
        pl.semaphore_signal(barrier, inc=1, device_id={"seq": me + 2}, device_id_type=MESH)

    @pl.when(pair >= 1)
    def _():
        pl.semaphore_signal(barrier, inc=1, device_id={"seq": me - 4}, device_id_type=MESH)

    @pl.when(pair + 1 < pairs)
    def _():
        pl.semaphore_signal(barrier, inc=1, device_id={"seq": me + 4}, device_id_type=MESH)

    greeted = [has_far, has_next, pair >= 1, pair + 1 < pairs]
    pl.semaphore_wait(barrier, 1 + sum(g.astype(jnp.int32) for g in greeted))

    def remote(src, dst, send, recv, h, to):
        return pltpu.make_async_remote_copy(
            src_ref=src.at[h], dst_ref=dst.at[h], send_sem=send.at[h], recv_sem=recv.at[h],
            device_id={"seq": to}, device_id_type=MESH,
        )

    def far_copy(h):
        return remote(own, far, far_send, far_recv, h, me + 2)

    def far_detour(h):
        return remote(own, relay, far_send, relay_recv, h, me + 4)

    def far_relay(h):
        return remote(relay, far, relay_send, far_recv, h, me - 2)

    def gfar_detour(h):
        return remote(gfar_out, relay, gfar_send, relay_recv, h, me - 4)

    def gfar_relay(h):
        return remote(relay, gfar_in, relay_send, gfar_recv, h, me + 2)

    def relay_forward(h):
        @pl.when(relays_forward(h))
        def _():
            far_detour(h).wait_recv()
            far_relay(h).start()

    def relay_back(h):
        @pl.when(relays_back(h))
        def _():
            gfar_detour(h).wait_recv()
            gfar_relay(h).start()

    def send_back(h):
        @pl.when(detours_back(h))
        def _():
            gfar_detour(h).start()

        @pl.when(jnp.logical_not(detours_back(h)))
        def _():
            gfar_copy(h).start()

    def near_own(h):
        return remote(own, near, near_send, near_recv, h, partner)

    def near_relay(h):
        return remote(far, near, near_send, near_recv, h, partner)

    def gnear_copy(h):
        return remote(gnear_out, gnear_in, gnear_send, gnear_recv, h, partner)

    def gfar_copy(h):
        return remote(gfar_out, gfar_in, gfar_send, gfar_recv, h, me - 2)

    loads[0].wait()
    loads[1].wait()
    loads[2].start()
    loads[3].start()

    def send_own(h, _):
        own[h, 0:tokens] = k_ref[pl.ds(h, tokens, stride=kheads), :].astype(BF16)
        own[h, tokens:] = v_ref[pl.ds(h, tokens, stride=kheads), :].astype(BF16)

        @pl.when(detours_forward(h))
        def _():
            far_detour(h).start()

        @pl.when(jnp.logical_and(has_next, jnp.logical_not(detours_forward(h))))
        def _():
            far_copy(h).start()

        @pl.when(core == 0)
        def _():
            near_own(h).start()

        return 0

    early = min(3, kheads)
    lax.fori_loop(0, early, send_own, 0)
    loads[2].wait()
    loads[3].wait()

    def block(kind, h, kv, emit):
        for jb in range(2):
            k = kv[h, jb * half:(jb + 1) * half]
            v = kv[h, tokens + jb * half:tokens + (jb + 1) * half]
            dk = dv = None
            for g in range(group):
                lo, hi = 0, tokens
                if kind == "own":
                    lo = jb * half
                elif kind == "far":
                    hi = (jb + 1) * half
                rows = slice(g * tokens + lo, g * tokens + hi)
                q = qb[rows]
                go = gb[rows]
                lse = lse_ref[pl.ds(h * group + g, 1), lo:hi]
                dots = dots_ref[pl.ds(h * group + g, 1), lo:hi]
                s = dot(k, q, 1, 1)
                p = jnp.exp2(s * (SCALE * LOG2E) - lse * LOG2E)
                if kind != "near":
                    kpos = lax.broadcasted_iota(jnp.int32, p.shape, 0) + jb * half
                    qpos = lax.broadcasted_iota(jnp.int32, p.shape, 1) + lo
                    keep = qpos >= kpos if kind == "own" else qpos < kpos
                    p = jnp.where(keep, p, 0.0)
                ds = (p * (dot(v, go, 1, 1) - dots)).astype(BF16)
                dv_term = dot(p.astype(BF16), go, 1, 0)
                dk_term = dot(ds, q, 1, 0)
                dv = dv_term if dv is None else dv + dv_term
                dk = dk_term if dk is None else dk + dk_term
                dq = dot(ds, k, 0, 0)
                if kind == "own" and jb == 0:
                    dq_acc[rows] = dq
                else:
                    dq_acc[rows] += dq
            emit(jb, dk * SCALE, dv)

    def send_sum(h):
        slot = lax.rem(h, 2)
        gnear_copy(h).wait_recv()
        gfar_out[h] = (held[slot] + gnear_in[h].astype(F32)).astype(BF16)
        send_back(h)

    def step(h, _):
        for later in (early, early + 1):
            @pl.when(2 * h + later < kheads)
            def _():
                send_own(2 * h + later, 0)

        @pl.when(jnp.logical_and(core == 1, has_far))
        def _():
            far_copy(h).wait_recv()
            near_relay(h).start()

        for g in range(group):
            rows = slice(g * tokens, (g + 1) * tokens)
            at = pl.ds(h * group + g, tokens, stride=qheads)
            qb[rows] = q_ref[at, :].astype(BF16)
            gb[rows] = g_ref[at, :].astype(BF16)

        def emit_own(jb, dk, dv):
            at = pl.ds(jb * half * kheads + h, half, stride=kheads)
            dk_ref[at, :] = dk
            dv_ref[at, :] = dv

        block("own", h, own, emit_own)

        @pl.when(h == 0)
        def _():
            relay_forward(0)

        @pl.when(h + 1 < kheads)
        def _():
            relay_forward(h + 1)

        @pl.when(has_near)
        def _():
            jax.lax.cond(
                core == 0,
                lambda: near_relay(h).wait_recv(),
                lambda: near_own(h).wait_recv(),
            )

            def emit_near(jb, dk, dv):
                gnear_out[h, jb * half:(jb + 1) * half] = dk.astype(BF16)
                gnear_out[h, tokens + jb * half:tokens + (jb + 1) * half] = dv.astype(BF16)

            block("near", h, near, emit_near)
            gnear_copy(h).start()

        @pl.when(has_far)
        def _():
            @pl.when(core == 0)
            def _():
                far_copy(h).wait_recv()

            slot = lax.rem(h, 2)

            @pl.when(jnp.logical_and(core == 1, h >= 1))
            def _():
                send_sum(h - 1)

            def emit_far(jb, dk, dv):
                held[slot, jb * half:(jb + 1) * half] = dk
                held[slot, tokens + jb * half:tokens + (jb + 1) * half] = dv

            block("far", h, far, emit_far)

            @pl.when(core == 0)
            def _():
                gfar_out[h] = held[slot].astype(BF16)
                send_back(h)

        for g in range(group):
            at = pl.ds(h * group + g, tokens, stride=qheads)
            dq_ref[at, :] = dq_acc[g * tokens:(g + 1) * tokens] * SCALE

        @pl.when(h >= 2)
        def _():
            relay_back(h - 2)

        return 0

    lax.fori_loop(0, kheads, step, 0)

    @pl.when(jnp.logical_and(core == 1, has_far))
    def _():
        send_sum(kheads - 1)

    store = pltpu.make_async_copy(dq_ref, dq_hbm, store_sem)
    store.start()
    for h in range(max(kheads - 2, 0), kheads):
        relay_back(h)

    def finish(h, _):
        at = pl.ds(h, tokens, stride=kheads)

        @pl.when(core == 0)
        def _():
            gnear_copy(h).wait_recv()
            dk_ref[at, :] += gnear_in[h, 0:tokens].astype(F32)
            dv_ref[at, :] += gnear_in[h, tokens:].astype(F32)

        @pl.when(has_next)
        def _():
            gfar_copy(h).wait_recv()
            dk_ref[at, :] += gfar_in[h, 0:tokens].astype(F32)
            dv_ref[at, :] += gfar_in[h, tokens:].astype(F32)

        return 0

    lax.fori_loop(0, kheads, finish, 0)

    def drain(h, _):
        @pl.when(has_next)
        def _():
            far_copy(h).wait_send()

        @pl.when(gets_near)
        def _():
            near_own(h).wait_send()

        @pl.when(has_near)
        def _():
            gnear_copy(h).wait_send()

        @pl.when(has_far)
        def _():
            gfar_copy(h).wait_send()

        @pl.when(jnp.logical_or(relays_forward(h), relays_back(h)))
        def _():
            far_relay(h).wait_send()

        return 0

    lax.fori_loop(0, kheads, drain, 0)
    store.wait()


def on_device(devices, query, key, value, gradient, logsumexp, dots):
    tokens, qheads, width = query.shape
    kheads = key.shape[1]
    group = qheads // kheads
    assert WINDOW == 2 * tokens and devices % 4 == 0
    flat_q = (tokens * qheads, width)
    flat_k = (tokens * kheads, width)
    message = pltpu.VMEM((kheads, 2 * tokens, width), BF16)
    anywhere = pl.BlockSpec(memory_space=pl.ANY)
    vmem = pl.BlockSpec(memory_space=pltpu.VMEM)
    sems = pltpu.SemaphoreType.DMA((kheads,))
    dq, dk, dv = pl.pallas_call(
        functools.partial(kernel, tokens, kheads, group, devices),
        out_shape=(
            jax.ShapeDtypeStruct(flat_q, F32),
            jax.ShapeDtypeStruct(flat_k, F32),
            jax.ShapeDtypeStruct(flat_k, F32),
        ),
        in_specs=[anywhere] * 4 + [vmem] * 2,
        out_specs=(anywhere, vmem, vmem),
        scratch_shapes=[
            pltpu.VMEM(flat_q, F32),
            pltpu.VMEM(flat_k, F32),
            pltpu.VMEM(flat_k, F32),
            pltpu.VMEM(flat_q, F32),
            pltpu.VMEM(flat_q, F32),
        ] + [message] * 8 + [
            pltpu.VMEM((2, 2 * tokens, width), F32),
            pltpu.VMEM((group * tokens, width), F32),
            pltpu.VMEM((group * tokens, width), BF16),
            pltpu.VMEM((group * tokens, width), BF16),
            pltpu.SemaphoreType.DMA((4,)),
            pltpu.SemaphoreType.DMA,
        ] + [sems] * 10,
        compiler_params=pltpu.CompilerParams(
            collective_id=0, has_side_effects=True, vmem_limit_bytes=58 * 2**20
        ),
        cost_estimate=pl.CostEstimate(
            flops=10 * qheads * tokens * WINDOW * width,
            bytes_accessed=(3 * qheads + 4 * kheads) * tokens * width * 4,
            transcendentals=qheads * tokens * WINDOW,
        ),
    )(
        query.reshape(flat_q), key.reshape(flat_k), value.reshape(flat_k),
        gradient.reshape(flat_q), logsumexp, dots,
    )
    return dq.reshape(query.shape), dk.reshape(key.shape), dv.reshape(value.shape)


def solution(mesh):
    return jax.shard_map(
        functools.partial(on_device, mesh.shape["seq"]),
        mesh=mesh,
        in_specs=(
            P("seq", "head", None),
            P("seq", "head", None),
            P("seq", "head", None),
            P("seq", "head", None),
            P("head", "seq"),
            P("head", "seq"),
        ),
        out_specs=(P("seq", "head", None), P("seq", "head", None), P("seq", "head", None)),
        check_vma=False,
    )
```

```python
import functools
import math

import jax
import jax.numpy as jnp
from jax import lax
from jax.experimental import pallas as pl
from jax.experimental.pallas import tpu as pltpu
from jax.sharding import PartitionSpec as P

WINDOW = 1024
QSCALE = 168
SCALE = QSCALE ** (-0.5)
LOG2E = math.log2(math.e)
MESH = pl.DeviceIdType.MESH
BF16 = jnp.bfloat16
F32 = jnp.float32


def dot(a, b, ca, cb):
    return lax.dot_general(a, b, (((ca,), (cb,)), ((), ())), preferred_element_type=F32)


def kernel(
    tokens, kheads, group, devices,
    q_hbm, k_hbm, v_hbm, g_hbm, lse_ref, dots_ref,
    dq_hbm, dk_ref, dv_ref,
    q_ref, k_ref, v_ref, g_ref, dq_ref,
    own, far, near, relay, gnear_out, gnear_in, gfar_out, gfar_in,
    held, dq_acc, qb, gb, qt, gt,
    load_sem, store_sem,
    far_send, far_recv, near_send, near_recv,
    gnear_send, gnear_recv, gfar_send, gfar_recv, relay_send, relay_recv,
):
    qheads = kheads * group
    half = tokens // 2
    me = lax.axis_index("seq")
    core = lax.rem(me, 2)
    partner = me + 1 - 2 * core
    has_far = me >= 2
    has_near = me >= 1
    has_next = me + 2 < devices
    gets_near = jnp.logical_or(core == 0, has_far)
    pairs = devices // 4
    pair = me // 4
    odd = lax.rem(me // 2, 2) == 1

    def picked(h, share):
        return lax.rem(h * share, pairs) < share

    def both(*terms):
        return functools.reduce(jnp.logical_and, terms)

    def detours_forward(h):
        return both(odd, has_next, picked(h + 3, pair + 1))

    def relays_forward(h):
        return both(odd, pair >= 1, picked(h + 3, pair))

    def detours_back(h):
        return both(jnp.logical_not(odd), pair >= 1, picked(h, pairs - pair))

    def relays_back(h):
        return both(jnp.logical_not(odd), pair + 1 < pairs, picked(h, pairs - pair - 1))

    loads = [
        pltpu.make_async_copy(src, dst, load_sem.at[n])
        for n, (src, dst) in enumerate(
            ((k_hbm, k_ref), (v_hbm, v_ref), (q_hbm, q_ref), (g_hbm, g_ref))
        )
    ]
    loads[0].start()
    loads[1].start()

    barrier = pltpu.get_barrier_semaphore()
    pl.semaphore_signal(barrier, inc=1, device_id={"seq": partner}, device_id_type=MESH)

    @pl.when(has_far)
    def _():
        pl.semaphore_signal(barrier, inc=1, device_id={"seq": me - 2}, device_id_type=MESH)

    @pl.when(has_next)
    def _():
        pl.semaphore_signal(barrier, inc=1, device_id={"seq": me + 2}, device_id_type=MESH)

    @pl.when(pair >= 1)
    def _():
        pl.semaphore_signal(barrier, inc=1, device_id={"seq": me - 4}, device_id_type=MESH)

    @pl.when(pair + 1 < pairs)
    def _():
        pl.semaphore_signal(barrier, inc=1, device_id={"seq": me + 4}, device_id_type=MESH)

    greeted = [has_far, has_next, pair >= 1, pair + 1 < pairs]
    pl.semaphore_wait(barrier, 1 + sum(g.astype(jnp.int32) for g in greeted))

    def remote(src, dst, send, recv, h, to):
        return pltpu.make_async_remote_copy(
            src_ref=src.at[h], dst_ref=dst.at[h], send_sem=send.at[h], recv_sem=recv.at[h],
            device_id={"seq": to}, device_id_type=MESH,
        )

    def far_copy(h):
        return remote(own, far, far_send, far_recv, h, me + 2)

    def far_detour(h):
        return remote(own, relay, far_send, relay_recv, h, me + 4)

    def far_relay(h):
        return remote(relay, far, relay_send, far_recv, h, me - 2)

    def gfar_detour(h):
        return remote(gfar_out, relay, gfar_send, relay_recv, h, me - 4)

    def gfar_relay(h):
        return remote(relay, gfar_in, relay_send, gfar_recv, h, me + 2)

    def relay_forward(h):
        @pl.when(relays_forward(h))
        def _():
            far_detour(h).wait_recv()
            far_relay(h).start()

    def relay_back(h):
        @pl.when(relays_back(h))
        def _():
            gfar_detour(h).wait_recv()
            gfar_relay(h).start()

    def send_back(h):
        @pl.when(detours_back(h))
        def _():
            gfar_detour(h).start()

        @pl.when(jnp.logical_not(detours_back(h)))
        def _():
            gfar_copy(h).start()

    def near_own(h):
        return remote(own, near, near_send, near_recv, h, partner)

    def near_relay(h):
        return remote(far, near, near_send, near_recv, h, partner)

    def gnear_copy(h):
        return remote(gnear_out, gnear_in, gnear_send, gnear_recv, h, partner)

    def gfar_copy(h):
        return remote(gfar_out, gfar_in, gfar_send, gfar_recv, h, me - 2)

    loads[0].wait()
    loads[1].wait()
    loads[2].start()
    loads[3].start()

    def send_own(h, _):
        own[h, 0:tokens] = k_ref[pl.ds(h, tokens, stride=kheads), :].astype(BF16)
        own[h, tokens:] = v_ref[pl.ds(h, tokens, stride=kheads), :].astype(BF16)

        @pl.when(detours_forward(h))
        def _():
            far_detour(h).start()

        @pl.when(jnp.logical_and(has_next, jnp.logical_not(detours_forward(h))))
        def _():
            far_copy(h).start()

        @pl.when(core == 0)
        def _():
            near_own(h).start()

        return 0

    early = min(3, kheads)
    lax.fori_loop(0, early, send_own, 0)
    loads[2].wait()
    loads[3].wait()

    def block(kind, h, kv, emit):
        halves = {"own": ((0, 1), (1,)), "near": ((0, 1), (0, 1)), "far": ((0,), (0, 1))}[kind]
        kt = kv[h, 0:tokens].T
        ps, dss = {}, {}

        def scores(jb, g):
            lo, hi = halves[jb][0] * half, (halves[jb][-1] + 1) * half
            cols = slice(g * tokens + lo, g * tokens + hi)
            k = kv[h, jb * half:(jb + 1) * half]
            v = kv[h, tokens + jb * half:tokens + (jb + 1) * half]
            lse = lse_ref[pl.ds(h * group + g, 1), lo:hi]
            dots = dots_ref[pl.ds(h * group + g, 1), lo:hi]
            s = dot(k, qt[:, cols], 1, 0)
            p = jnp.exp2(s * (SCALE * LOG2E) - lse * LOG2E)
            if kind != "near":
                kpos = lax.broadcasted_iota(jnp.int32, p.shape, 0) + jb * half
                qpos = lax.broadcasted_iota(jnp.int32, p.shape, 1) + lo
                keep = qpos >= kpos if kind == "own" else qpos < kpos
                p = jnp.where(keep, p, 0.0)
            ds = p * (dot(v, gt[:, cols], 1, 0) - dots)
            ps[jb, g] = p.astype(BF16)
            dss[jb, g] = ds.astype(BF16)

        def key_terms(jb):
            lo, hi = halves[jb][0] * half, (halves[jb][-1] + 1) * half
            rows = [slice(g * tokens + lo, g * tokens + hi) for g in range(group)]
            p = jnp.concatenate([ps[jb, g] for g in range(group)], axis=1)
            ds = jnp.concatenate([dss[jb, g] for g in range(group)], axis=1)
            go = jnp.concatenate([gb[r] for r in rows], axis=0)
            q = jnp.concatenate([qb[r] for r in rows], axis=0)
            emit(jb, dot(ds, q, 1, 0) * SCALE, dot(p, go, 1, 0))

        def query_terms(g):
            for ib in range(2):
                jbs = [jb for jb in range(2) if ib in halves[jb]]
                parts = []
                for jb in jbs:
                    at = (ib - halves[jb][0]) * half
                    parts.append(dss[jb, g][:, at:at + half])
                ds = parts[0] if len(parts) == 1 else jnp.concatenate(parts, axis=0)
                dq = dot(kt[:, jbs[0] * half:(jbs[-1] + 1) * half], ds, 1, 0)
                cols = slice(g * tokens + ib * half, g * tokens + (ib + 1) * half)
                if kind == "own":
                    dq_acc[:, cols] = dq
                else:
                    dq_acc[:, cols] += dq

        for g in range(group):
            scores(0, g)
        scores(1, 0)
        key_terms(0)
        for g in range(1, group):
            scores(1, g)
        query_terms(0)
        key_terms(1)
        for g in range(1, group):
            query_terms(g)

    def send_sum(h):
        slot = lax.rem(h, 2)
        gnear_copy(h).wait_recv()
        gfar_out[h] = (held[slot] + gnear_in[h].astype(F32)).astype(BF16)
        send_back(h)

    def step(h, _):
        for later in (early, early + 1):
            @pl.when(2 * h + later < kheads)
            def _():
                send_own(2 * h + later, 0)

        @pl.when(jnp.logical_and(core == 1, has_far))
        def _():
            far_copy(h).wait_recv()
            near_relay(h).start()

        for g in range(group):
            rows = slice(g * tokens, (g + 1) * tokens)
            at = pl.ds(h * group + g, tokens, stride=qheads)
            q = q_ref[at, :]
            go = g_ref[at, :]
            qb[rows] = q.astype(BF16)
            gb[rows] = go.astype(BF16)
            qt[:, rows] = q.T.astype(BF16)
            gt[:, rows] = go.T.astype(BF16)

        def emit_own(jb, dk, dv):
            at = pl.ds(jb * half * kheads + h, half, stride=kheads)
            dk_ref[at, :] = dk
            dv_ref[at, :] = dv

        block("own", h, own, emit_own)

        @pl.when(h == 0)
        def _():
            relay_forward(0)

        @pl.when(h + 1 < kheads)
        def _():
            relay_forward(h + 1)

        @pl.when(has_near)
        def _():
            jax.lax.cond(
                core == 0,
                lambda: near_relay(h).wait_recv(),
                lambda: near_own(h).wait_recv(),
            )

            def emit_near(jb, dk, dv):
                gnear_out[h, jb * half:(jb + 1) * half] = dk.astype(BF16)
                gnear_out[h, tokens + jb * half:tokens + (jb + 1) * half] = dv.astype(BF16)

            block("near", h, near, emit_near)
            gnear_copy(h).start()

        @pl.when(has_far)
        def _():
            @pl.when(core == 0)
            def _():
                far_copy(h).wait_recv()

            slot = lax.rem(h, 2)

            @pl.when(jnp.logical_and(core == 1, h >= 1))
            def _():
                send_sum(h - 1)

            def emit_far(jb, dk, dv):
                held[slot, jb * half:(jb + 1) * half] = dk
                held[slot, tokens + jb * half:tokens + (jb + 1) * half] = dv

            block("far", h, far, emit_far)

            @pl.when(core == 0)
            def _():
                gfar_out[h] = held[slot].astype(BF16)
                send_back(h)

        for g in range(group):
            at = pl.ds(h * group + g, tokens, stride=qheads)
            dq_ref[at, :] = dq_acc[:, g * tokens:(g + 1) * tokens].T * SCALE

        @pl.when(h >= 2)
        def _():
            relay_back(h - 2)

        return 0

    lax.fori_loop(0, kheads, step, 0)

    @pl.when(jnp.logical_and(core == 1, has_far))
    def _():
        send_sum(kheads - 1)

    store = pltpu.make_async_copy(dq_ref, dq_hbm, store_sem)
    store.start()
    for h in range(max(kheads - 2, 0), kheads):
        relay_back(h)

    def finish(h, _):
        at = pl.ds(h, tokens, stride=kheads)

        @pl.when(core == 0)
        def _():
            gnear_copy(h).wait_recv()
            dk_ref[at, :] += gnear_in[h, 0:tokens].astype(F32)
            dv_ref[at, :] += gnear_in[h, tokens:].astype(F32)

        @pl.when(has_next)
        def _():
            gfar_copy(h).wait_recv()
            dk_ref[at, :] += gfar_in[h, 0:tokens].astype(F32)
            dv_ref[at, :] += gfar_in[h, tokens:].astype(F32)

        return 0

    lax.fori_loop(0, kheads, finish, 0)

    def drain(h, _):
        @pl.when(has_next)
        def _():
            far_copy(h).wait_send()

        @pl.when(gets_near)
        def _():
            near_own(h).wait_send()

        @pl.when(has_near)
        def _():
            gnear_copy(h).wait_send()

        @pl.when(has_far)
        def _():
            gfar_copy(h).wait_send()

        @pl.when(jnp.logical_or(relays_forward(h), relays_back(h)))
        def _():
            far_relay(h).wait_send()

        return 0

    lax.fori_loop(0, kheads, drain, 0)
    store.wait()


def on_device(devices, query, key, value, gradient, logsumexp, dots):
    tokens, qheads, width = query.shape
    kheads = key.shape[1]
    group = qheads // kheads
    assert WINDOW == 2 * tokens and devices % 4 == 0
    flat_q = (tokens * qheads, width)
    flat_k = (tokens * kheads, width)
    message = pltpu.VMEM((kheads, 2 * tokens, width), BF16)
    anywhere = pl.BlockSpec(memory_space=pl.ANY)
    vmem = pl.BlockSpec(memory_space=pltpu.VMEM)
    sems = pltpu.SemaphoreType.DMA((kheads,))
    dq, dk, dv = pl.pallas_call(
        functools.partial(kernel, tokens, kheads, group, devices),
        out_shape=(
            jax.ShapeDtypeStruct(flat_q, F32),
            jax.ShapeDtypeStruct(flat_k, F32),
            jax.ShapeDtypeStruct(flat_k, F32),
        ),
        in_specs=[anywhere] * 4 + [vmem] * 2,
        out_specs=(anywhere, vmem, vmem),
        scratch_shapes=[
            pltpu.VMEM(flat_q, F32),
            pltpu.VMEM(flat_k, F32),
            pltpu.VMEM(flat_k, F32),
            pltpu.VMEM(flat_q, F32),
            pltpu.VMEM(flat_q, F32),
        ] + [message] * 8 + [
            pltpu.VMEM((2, 2 * tokens, width), F32),
            pltpu.VMEM((width, group * tokens), F32),
            pltpu.VMEM((group * tokens, width), BF16),
            pltpu.VMEM((group * tokens, width), BF16),
            pltpu.VMEM((width, group * tokens), BF16),
            pltpu.VMEM((width, group * tokens), BF16),
            pltpu.SemaphoreType.DMA((4,)),
            pltpu.SemaphoreType.DMA,
        ] + [sems] * 10,
        compiler_params=pltpu.CompilerParams(
            collective_id=0, has_side_effects=True, vmem_limit_bytes=58 * 2**20
        ),
        cost_estimate=pl.CostEstimate(
            flops=10 * qheads * tokens * WINDOW * width,
            bytes_accessed=(3 * qheads + 4 * kheads) * tokens * width * 4,
            transcendentals=qheads * tokens * WINDOW,
        ),
    )(
        query.reshape(flat_q), key.reshape(flat_k), value.reshape(flat_k),
        gradient.reshape(flat_q), logsumexp, dots,
    )
    return dq.reshape(query.shape), dk.reshape(key.shape), dv.reshape(value.shape)


def solution(mesh):
    return jax.shard_map(
        functools.partial(on_device, mesh.shape["seq"]),
        mesh=mesh,
        in_specs=(
            P("seq", "head", None),
            P("seq", "head", None),
            P("seq", "head", None),
            P("seq", "head", None),
            P("head", "seq"),
            P("head", "seq"),
        ),
        out_specs=(P("seq", "head", None), P("seq", "head", None), P("seq", "head", None)),
        check_vma=False,
    )
```

```python
import functools
import math

import jax
import jax.numpy as jnp
from jax import lax
from jax.experimental import pallas as pl
from jax.experimental.pallas import tpu as pltpu
from jax.sharding import PartitionSpec as P

WINDOW = 1024
QSCALE = 168
SCALE = QSCALE ** (-0.5)
LOG2E = math.log2(math.e)
MESH = pl.DeviceIdType.MESH
BF16 = jnp.bfloat16
F32 = jnp.float32


def dot(a, b, ca, cb):
    return lax.dot_general(a, b, (((ca,), (cb,)), ((), ())), preferred_element_type=F32)


def kernel(
    tokens, kheads, group, devices,
    q_hbm, k_hbm, v_hbm, g_hbm, lse_ref, dots_ref,
    dq_hbm, dk_out, dv_out,
    q_ref, k_ref, v_ref, g_ref, dq_ref, dk_ref, dv_ref, dq_low,
    own, far, near, relay, gnear_out, gnear_in, gfar_out, gfar_in,
    held, dq_acc, qb, gb, qt, gt,
    load_sem, store_sem,
    far_send, far_recv, near_send, near_recv,
    gnear_send, gnear_recv, gfar_send, gfar_recv, relay_send, relay_recv,
):
    qheads = kheads * group
    half = tokens // 2
    me = lax.axis_index("seq")
    core = lax.rem(me, 2)
    partner = me + 1 - 2 * core
    has_far = me >= 2
    has_near = me >= 1
    has_next = me + 2 < devices
    gets_near = jnp.logical_or(core == 0, has_far)
    pairs = devices // 4
    pair = me // 4
    odd = lax.rem(me // 2, 2) == 1

    def picked(h, share):
        return lax.rem(h * share, pairs) < share

    def both(*terms):
        return functools.reduce(jnp.logical_and, terms)

    def detours_forward(h):
        return both(odd, has_next, picked(h + 3, pair + 1))

    def relays_forward(h):
        return both(odd, pair >= 1, picked(h + 3, pair))

    def detours_back(h):
        return both(jnp.logical_not(odd), pair >= 1, picked(h, pairs - pair))

    def relays_back(h):
        return both(jnp.logical_not(odd), pair + 1 < pairs, picked(h, pairs - pair - 1))

    loads = [
        pltpu.make_async_copy(src, dst, load_sem.at[n])
        for n, (src, dst) in enumerate(
            ((k_hbm, k_ref), (v_hbm, v_ref), (q_hbm, q_ref), (g_hbm, g_ref))
        )
    ]
    loads[0].start()
    loads[1].start()

    barrier = pltpu.get_barrier_semaphore()
    pl.semaphore_signal(barrier, inc=1, device_id={"seq": partner}, device_id_type=MESH)

    @pl.when(has_far)
    def _():
        pl.semaphore_signal(barrier, inc=1, device_id={"seq": me - 2}, device_id_type=MESH)

    @pl.when(has_next)
    def _():
        pl.semaphore_signal(barrier, inc=1, device_id={"seq": me + 2}, device_id_type=MESH)

    @pl.when(pair >= 1)
    def _():
        pl.semaphore_signal(barrier, inc=1, device_id={"seq": me - 4}, device_id_type=MESH)

    @pl.when(pair + 1 < pairs)
    def _():
        pl.semaphore_signal(barrier, inc=1, device_id={"seq": me + 4}, device_id_type=MESH)

    greeted = [has_far, has_next, pair >= 1, pair + 1 < pairs]
    pl.semaphore_wait(barrier, 1 + sum(g.astype(jnp.int32) for g in greeted))

    def remote(src, dst, send, recv, h, to):
        return pltpu.make_async_remote_copy(
            src_ref=src.at[h], dst_ref=dst.at[h], send_sem=send.at[h], recv_sem=recv.at[h],
            device_id={"seq": to}, device_id_type=MESH,
        )

    def far_copy(h):
        return remote(own, far, far_send, far_recv, h, me + 2)

    def far_detour(h):
        return remote(own, relay, far_send, relay_recv, h, me + 4)

    def far_relay(h):
        return remote(relay, far, relay_send, far_recv, h, me - 2)

    def gfar_detour(h):
        return remote(gfar_out, relay, gfar_send, relay_recv, h, me - 4)

    def gfar_relay(h):
        return remote(relay, gfar_in, relay_send, gfar_recv, h, me + 2)

    def relay_forward(h):
        @pl.when(relays_forward(h))
        def _():
            far_detour(h).wait_recv()
            far_relay(h).start()

    def relay_back(h):
        @pl.when(relays_back(h))
        def _():
            gfar_detour(h).wait_recv()
            gfar_relay(h).start()

    def send_back(h):
        @pl.when(detours_back(h))
        def _():
            gfar_detour(h).start()

        @pl.when(jnp.logical_not(detours_back(h)))
        def _():
            gfar_copy(h).start()

    def near_own(h):
        return remote(own, near, near_send, near_recv, h, partner)

    def near_relay(h):
        return remote(far, near, near_send, near_recv, h, partner)

    def gnear_copy(h):
        return remote(gnear_out, gnear_in, gnear_send, gnear_recv, h, partner)

    def gfar_copy(h):
        return remote(gfar_out, gfar_in, gfar_send, gfar_recv, h, me - 2)

    loads[0].wait()
    loads[1].wait()
    loads[2].start()
    loads[3].start()

    def send_own(h, _):
        own[h, 0:tokens] = k_ref[pl.ds(h, tokens, stride=kheads), :].astype(BF16)
        own[h, tokens:] = v_ref[pl.ds(h, tokens, stride=kheads), :].astype(BF16)

        @pl.when(detours_forward(h))
        def _():
            far_detour(h).start()

        @pl.when(jnp.logical_and(has_next, jnp.logical_not(detours_forward(h))))
        def _():
            far_copy(h).start()

        @pl.when(core == 0)
        def _():
            near_own(h).start()

        return 0

    lax.fori_loop(0, kheads, send_own, 0)
    loads[2].wait()
    loads[3].wait()

    def block(kind, h, kv, emit):
        halves = {"own": ((0, 1), (1,)), "near": ((0, 1), (0, 1)), "far": ((0,), (0, 1))}[kind]
        kt = kv[h, 0:tokens].T
        ps, dss = {}, {}

        def scores(jb, g):
            lo, hi = halves[jb][0] * half, (halves[jb][-1] + 1) * half
            cols = slice(g * tokens + lo, g * tokens + hi)
            k = kv[h, jb * half:(jb + 1) * half]
            v = kv[h, tokens + jb * half:tokens + (jb + 1) * half]
            lse = lse_ref[pl.ds(h * group + g, 1), lo:hi]
            dots = dots_ref[pl.ds(h * group + g, 1), lo:hi]
            s = dot(k, qt[:, cols], 1, 0)
            p = jnp.exp2(s * (SCALE * LOG2E) - lse * LOG2E)
            if kind != "near":
                kpos = lax.broadcasted_iota(jnp.int32, p.shape, 0) + jb * half
                qpos = lax.broadcasted_iota(jnp.int32, p.shape, 1) + lo
                keep = qpos >= kpos if kind == "own" else qpos < kpos
                p = jnp.where(keep, p, 0.0)
            ds = p * (dot(v, gt[:, cols], 1, 0) - dots)
            ps[jb, g] = p.astype(BF16)
            dss[jb, g] = ds.astype(BF16)

        def key_terms(jb):
            lo, hi = halves[jb][0] * half, (halves[jb][-1] + 1) * half
            rows = [slice(g * tokens + lo, g * tokens + hi) for g in range(group)]
            p = jnp.concatenate([ps[jb, g] for g in range(group)], axis=1)
            ds = jnp.concatenate([dss[jb, g] for g in range(group)], axis=1)
            go = jnp.concatenate([gb[r] for r in rows], axis=0)
            q = jnp.concatenate([qb[r] for r in rows], axis=0)
            emit(jb, dot(ds, q, 1, 0) * SCALE, dot(p, go, 1, 0))

        def query_terms(g):
            for ib in range(2):
                jbs = [jb for jb in range(2) if ib in halves[jb]]
                parts = []
                for jb in jbs:
                    at = (ib - halves[jb][0]) * half
                    parts.append(dss[jb, g][:, at:at + half])
                ds = parts[0] if len(parts) == 1 else jnp.concatenate(parts, axis=0)
                dq = dot(kt[:, jbs[0] * half:(jbs[-1] + 1) * half], ds, 1, 0)
                cols = slice(g * tokens + ib * half, g * tokens + (ib + 1) * half)
                if kind == "own":
                    dq_acc[:, cols] = dq
                else:
                    dq_acc[:, cols] += dq

        for g in range(group):
            scores(0, g)
        scores(1, 0)
        key_terms(0)
        for g in range(1, group):
            scores(1, g)
        query_terms(0)
        key_terms(1)
        for g in range(1, group):
            query_terms(g)

    def send_sum(h):
        slot = lax.rem(h, 2)
        gnear_copy(h).wait_recv()
        gfar_out[h] = (held[slot] + gnear_in[h].astype(F32)).astype(BF16)
        send_back(h)

    def step(h, _):
        @pl.when(jnp.logical_and(core == 1, has_far))
        def _():
            far_copy(h).wait_recv()
            near_relay(h).start()

        for g in range(group):
            rows = slice(g * tokens, (g + 1) * tokens)
            at = pl.ds(h * group + g, tokens, stride=qheads)
            q = q_ref[at, :]
            go = g_ref[at, :]
            qb[rows] = q.astype(BF16)
            gb[rows] = go.astype(BF16)
            qt[:, rows] = q.T.astype(BF16)
            gt[:, rows] = go.T.astype(BF16)

        def emit_own(jb, dk, dv):
            at = pl.ds(jb * half * kheads + h, half, stride=kheads)
            dk_ref[at, :] = dk
            dv_ref[at, :] = dv

        block("own", h, own, emit_own)

        @pl.when(h == 0)
        def _():
            relay_forward(0)

        @pl.when(h + 1 < kheads)
        def _():
            relay_forward(h + 1)

        @pl.when(has_near)
        def _():
            jax.lax.cond(
                core == 0,
                lambda: near_relay(h).wait_recv(),
                lambda: near_own(h).wait_recv(),
            )

            def emit_near(jb, dk, dv):
                gnear_out[h, jb * half:(jb + 1) * half] = dk.astype(BF16)
                gnear_out[h, tokens + jb * half:tokens + (jb + 1) * half] = dv.astype(BF16)

            block("near", h, near, emit_near)
            gnear_copy(h).start()

        @pl.when(has_far)
        def _():
            @pl.when(core == 0)
            def _():
                far_copy(h).wait_recv()

            slot = lax.rem(h, 2)

            @pl.when(jnp.logical_and(core == 1, h >= 1))
            def _():
                send_sum(h - 1)

            def emit_far(jb, dk, dv):
                held[slot, jb * half:(jb + 1) * half] = dk
                held[slot, tokens + jb * half:tokens + (jb + 1) * half] = dv

            block("far", h, far, emit_far)

            @pl.when(core == 0)
            def _():
                gfar_out[h] = held[slot].astype(BF16)
                send_back(h)

        for g in range(group):
            at = pl.ds(h * group + g, tokens, stride=qheads)
            dq_ref[at, :] = dq_acc[:, g * tokens:(g + 1) * tokens].T * SCALE

        @pl.when(h >= 2)
        def _():
            relay_back(h - 2)

        return 0

    lax.fori_loop(0, kheads, step, 0)

    @pl.when(jnp.logical_and(core == 1, has_far))
    def _():
        send_sum(kheads - 1)

    for h in range(max(kheads - 2, 0), kheads):
        relay_back(h)

    def round_query(n, _):
        rows = pl.ds(pl.multiple_of(n * tokens, tokens), tokens)
        dq_low[rows] = dq_ref[rows].astype(BF16)
        return 0

    lax.fori_loop(0, qheads, round_query, 0)
    store = pltpu.make_async_copy(dq_low, dq_hbm, store_sem)
    store.start()

    def finish(h, _):
        at = pl.ds(h, tokens, stride=kheads)

        @pl.when(core == 0)
        def _():
            gnear_copy(h).wait_recv()
            dk_ref[at, :] += gnear_in[h, 0:tokens].astype(F32)
            dv_ref[at, :] += gnear_in[h, tokens:].astype(F32)

        @pl.when(has_next)
        def _():
            gfar_copy(h).wait_recv()
            dk_ref[at, :] += gfar_in[h, 0:tokens].astype(F32)
            dv_ref[at, :] += gfar_in[h, tokens:].astype(F32)

        return 0

    lax.fori_loop(0, kheads, finish, 0)

    def round_keys(n, _):
        rows = pl.ds(pl.multiple_of(n * tokens, tokens), tokens)
        dk_out[rows] = dk_ref[rows].astype(BF16)
        dv_out[rows] = dv_ref[rows].astype(BF16)
        return 0

    lax.fori_loop(0, kheads, round_keys, 0)

    def drain(h, _):
        @pl.when(has_next)
        def _():
            far_copy(h).wait_send()

        @pl.when(gets_near)
        def _():
            near_own(h).wait_send()

        @pl.when(has_near)
        def _():
            gnear_copy(h).wait_send()

        @pl.when(has_far)
        def _():
            gfar_copy(h).wait_send()

        @pl.when(jnp.logical_or(relays_forward(h), relays_back(h)))
        def _():
            far_relay(h).wait_send()

        return 0

    lax.fori_loop(0, kheads, drain, 0)
    store.wait()


def on_device(devices, query, key, value, gradient, logsumexp, dots):
    tokens, qheads, width = query.shape
    kheads = key.shape[1]
    group = qheads // kheads
    assert WINDOW == 2 * tokens and devices % 4 == 0
    flat_q = (tokens * qheads, width)
    flat_k = (tokens * kheads, width)
    message = pltpu.VMEM((kheads, 2 * tokens, width), BF16)
    anywhere = pl.BlockSpec(memory_space=pl.ANY)
    vmem = pl.BlockSpec(memory_space=pltpu.VMEM)
    sems = pltpu.SemaphoreType.DMA((kheads,))
    dq, dk, dv = pl.pallas_call(
        functools.partial(kernel, tokens, kheads, group, devices),
        out_shape=(
            jax.ShapeDtypeStruct(flat_q, BF16),
            jax.ShapeDtypeStruct(flat_k, BF16),
            jax.ShapeDtypeStruct(flat_k, BF16),
        ),
        in_specs=[anywhere] * 4 + [vmem] * 2,
        out_specs=(anywhere, vmem, vmem),
        scratch_shapes=[
            pltpu.VMEM(flat_q, F32),
            pltpu.VMEM(flat_k, F32),
            pltpu.VMEM(flat_k, F32),
            pltpu.VMEM(flat_q, F32),
            pltpu.VMEM(flat_q, F32),
            pltpu.VMEM(flat_k, F32),
            pltpu.VMEM(flat_k, F32),
            pltpu.VMEM(flat_q, BF16),
        ] + [message] * 8 + [
            pltpu.VMEM((2, 2 * tokens, width), F32),
            pltpu.VMEM((width, group * tokens), F32),
            pltpu.VMEM((group * tokens, width), BF16),
            pltpu.VMEM((group * tokens, width), BF16),
            pltpu.VMEM((width, group * tokens), BF16),
            pltpu.VMEM((width, group * tokens), BF16),
            pltpu.SemaphoreType.DMA((4,)),
            pltpu.SemaphoreType.DMA,
        ] + [sems] * 10,
        compiler_params=pltpu.CompilerParams(
            collective_id=0, has_side_effects=True, vmem_limit_bytes=58 * 2**20
        ),
        cost_estimate=pl.CostEstimate(
            flops=10 * qheads * tokens * WINDOW * width,
            bytes_accessed=(3 * qheads + 4 * kheads) * tokens * width * 4,
            transcendentals=qheads * tokens * WINDOW,
        ),
    )(
        query.reshape(flat_q), key.reshape(flat_k), value.reshape(flat_k),
        gradient.reshape(flat_q), logsumexp, dots,
    )
    return (
        dq.astype(F32).reshape(query.shape),
        dk.astype(F32).reshape(key.shape),
        dv.astype(F32).reshape(value.shape),
    )


def solution(mesh):
    return jax.shard_map(
        functools.partial(on_device, mesh.shape["seq"]),
        mesh=mesh,
        in_specs=(
            P("seq", "head", None),
            P("seq", "head", None),
            P("seq", "head", None),
            P("seq", "head", None),
            P("head", "seq"),
            P("head", "seq"),
        ),
        out_specs=(P("seq", "head", None), P("seq", "head", None), P("seq", "head", None)),
        check_vma=False,
    )
```

```python
import functools
import math

import jax
import jax.numpy as jnp
from jax import lax
from jax.experimental import pallas as pl
from jax.experimental.pallas import tpu as pltpu
from jax.sharding import PartitionSpec as P

WINDOW = 1024
QSCALE = 168
SCALE = QSCALE ** (-0.5)
LOG2E = math.log2(math.e)
MESH = pl.DeviceIdType.MESH
BF16 = jnp.bfloat16
F32 = jnp.float32


def dot(a, b, ca, cb):
    return lax.dot_general(a, b, (((ca,), (cb,)), ((), ())), preferred_element_type=F32)


def kernel(
    tokens, kheads, group, devices,
    q_hbm, k_hbm, v_hbm, g_hbm, lse_ref, dots_ref,
    dq_hbm, dk_out, dv_out,
    q_ref, k_ref, v_ref, g_ref, dq_ref, dk_ref, dv_ref, dq_low,
    own, far, near, relay, gnear_out, gnear_in, gfar_out, gfar_in,
    held, dq_acc, qb, gb, qt, gt,
    load_sem, store_sem,
    far_send, far_recv, near_send, near_recv,
    gnear_send, gnear_recv, gfar_send, gfar_recv, relay_send, relay_recv,
):
    qheads = kheads * group
    half = tokens // 2
    me = lax.axis_index("seq")
    core = lax.rem(me, 2)
    partner = me + 1 - 2 * core
    has_far = me >= 2
    has_near = me >= 1
    has_next = me + 2 < devices
    gets_near = jnp.logical_or(core == 0, has_far)
    pairs = devices // 4
    pair = me // 4
    odd = lax.rem(me // 2, 2) == 1

    def picked(h, share):
        return lax.rem(h * share, pairs) < share

    def both(*terms):
        return functools.reduce(jnp.logical_and, terms)

    def detours_forward(h):
        return both(odd, has_next, picked(h + 3, pair + 1))

    def relays_forward(h):
        return both(odd, pair >= 1, picked(h + 3, pair))

    def detours_back(h):
        return both(jnp.logical_not(odd), pair >= 1, picked(h, jnp.minimum(pairs - pair, pairs // 2)))

    def relays_back(h):
        return both(jnp.logical_not(odd), pair + 1 < pairs, picked(h, jnp.minimum(pairs - pair - 1, pairs // 2)))

    loads = [
        pltpu.make_async_copy(src, dst, load_sem.at[n])
        for n, (src, dst) in enumerate(
            ((k_hbm, k_ref), (v_hbm, v_ref), (q_hbm, q_ref), (g_hbm, g_ref))
        )
    ]
    loads[0].start()
    loads[1].start()

    barrier = pltpu.get_barrier_semaphore()
    pl.semaphore_signal(barrier, inc=1, device_id={"seq": partner}, device_id_type=MESH)

    @pl.when(has_far)
    def _():
        pl.semaphore_signal(barrier, inc=1, device_id={"seq": me - 2}, device_id_type=MESH)

    @pl.when(has_next)
    def _():
        pl.semaphore_signal(barrier, inc=1, device_id={"seq": me + 2}, device_id_type=MESH)

    @pl.when(pair >= 1)
    def _():
        pl.semaphore_signal(barrier, inc=1, device_id={"seq": me - 4}, device_id_type=MESH)

    @pl.when(pair + 1 < pairs)
    def _():
        pl.semaphore_signal(barrier, inc=1, device_id={"seq": me + 4}, device_id_type=MESH)

    greeted = [has_far, has_next, pair >= 1, pair + 1 < pairs]
    pl.semaphore_wait(barrier, 1 + sum(g.astype(jnp.int32) for g in greeted))

    def remote(src, dst, send, recv, h, to):
        return pltpu.make_async_remote_copy(
            src_ref=src.at[h], dst_ref=dst.at[h], send_sem=send.at[h], recv_sem=recv.at[h],
            device_id={"seq": to}, device_id_type=MESH,
        )

    def far_copy(h):
        return remote(own, far, far_send, far_recv, h, me + 2)

    def far_detour(h):
        return remote(own, relay, far_send, relay_recv, h, me + 4)

    def far_relay(h):
        return remote(relay, far, relay_send, far_recv, h, me - 2)

    def gfar_detour(h):
        return remote(gfar_out, relay, gfar_send, relay_recv, h, me - 4)

    def gfar_relay(h):
        return remote(relay, gfar_in, relay_send, gfar_recv, h, me + 2)

    def relay_forward(h):
        @pl.when(relays_forward(h))
        def _():
            far_detour(h).wait_recv()
            far_relay(h).start()

    def relay_back(h):
        @pl.when(relays_back(h))
        def _():
            gfar_detour(h).wait_recv()
            gfar_relay(h).start()

    def send_back(h):
        @pl.when(detours_back(h))
        def _():
            gfar_detour(h).start()

        @pl.when(jnp.logical_not(detours_back(h)))
        def _():
            gfar_copy(h).start()

    def near_own(h):
        return remote(own, near, near_send, near_recv, h, partner)

    def near_relay(h):
        return remote(far, near, near_send, near_recv, h, partner)

    def gnear_copy(h):
        return remote(gnear_out, gnear_in, gnear_send, gnear_recv, h, partner)

    def gfar_copy(h):
        return remote(gfar_out, gfar_in, gfar_send, gfar_recv, h, me - 2)

    loads[0].wait()
    loads[1].wait()
    loads[2].start()
    loads[3].start()

    def send_own(h, _):
        own[h, 0:tokens] = k_ref[pl.ds(h, tokens, stride=kheads), :].astype(BF16)
        own[h, tokens:] = v_ref[pl.ds(h, tokens, stride=kheads), :].astype(BF16)

        @pl.when(detours_forward(h))
        def _():
            far_detour(h).start()

        @pl.when(jnp.logical_and(has_next, jnp.logical_not(detours_forward(h))))
        def _():
            far_copy(h).start()

        @pl.when(core == 0)
        def _():
            near_own(h).start()

        return 0

    lax.fori_loop(0, kheads, send_own, 0)
    loads[2].wait()
    loads[3].wait()

    def block(kind, h, kv, emit):
        halves = {"own": ((0, 1), (1,)), "near": ((0, 1), (0, 1)), "far": ((0,), (0, 1))}[kind]
        kt = kv[h, 0:tokens].T
        ps, dss = {}, {}

        def scores(jb, g):
            lo, hi = halves[jb][0] * half, (halves[jb][-1] + 1) * half
            cols = slice(g * tokens + lo, g * tokens + hi)
            k = kv[h, jb * half:(jb + 1) * half]
            v = kv[h, tokens + jb * half:tokens + (jb + 1) * half]
            lse = lse_ref[pl.ds(h * group + g, 1), lo:hi]
            dots = dots_ref[pl.ds(h * group + g, 1), lo:hi]
            s = dot(k, qt[:, cols], 1, 0)
            p = jnp.exp2(s * (SCALE * LOG2E) - lse * LOG2E)
            if kind != "near":
                kpos = lax.broadcasted_iota(jnp.int32, p.shape, 0) + jb * half
                qpos = lax.broadcasted_iota(jnp.int32, p.shape, 1) + lo
                keep = qpos >= kpos if kind == "own" else qpos < kpos
                p = jnp.where(keep, p, 0.0)
            ds = p * (dot(v, gt[:, cols], 1, 0) - dots)
            ps[jb, g] = p.astype(BF16)
            dss[jb, g] = ds.astype(BF16)

        def key_terms(jb):
            lo, hi = halves[jb][0] * half, (halves[jb][-1] + 1) * half
            rows = [slice(g * tokens + lo, g * tokens + hi) for g in range(group)]
            p = jnp.concatenate([ps[jb, g] for g in range(group)], axis=1)
            ds = jnp.concatenate([dss[jb, g] for g in range(group)], axis=1)
            go = jnp.concatenate([gb[r] for r in rows], axis=0)
            q = jnp.concatenate([qb[r] for r in rows], axis=0)
            emit(jb, dot(ds, q, 1, 0) * SCALE, dot(p, go, 1, 0))

        def query_terms(g):
            for ib in range(2):
                jbs = [jb for jb in range(2) if ib in halves[jb]]
                parts = []
                for jb in jbs:
                    at = (ib - halves[jb][0]) * half
                    parts.append(dss[jb, g][:, at:at + half])
                ds = parts[0] if len(parts) == 1 else jnp.concatenate(parts, axis=0)
                dq = dot(kt[:, jbs[0] * half:(jbs[-1] + 1) * half], ds, 1, 0)
                cols = slice(g * tokens + ib * half, g * tokens + (ib + 1) * half)
                if kind == "own":
                    dq_acc[:, cols] = dq
                else:
                    dq_acc[:, cols] += dq

        for g in range(group):
            scores(0, g)
        scores(1, 0)
        key_terms(0)
        for g in range(1, group):
            scores(1, g)
        query_terms(0)
        key_terms(1)
        for g in range(1, group):
            query_terms(g)

    def send_sum(h):
        slot = lax.rem(h, 2)
        gnear_copy(h).wait_recv()
        gfar_out[h] = (held[slot] + gnear_in[h].astype(F32)).astype(BF16)
        send_back(h)

    def step(h, _):
        @pl.when(jnp.logical_and(core == 1, has_far))
        def _():
            far_copy(h).wait_recv()
            near_relay(h).start()

        for g in range(group):
            rows = slice(g * tokens, (g + 1) * tokens)
            at = pl.ds(h * group + g, tokens, stride=qheads)
            q = q_ref[at, :]
            go = g_ref[at, :]
            qb[rows] = q.astype(BF16)
            gb[rows] = go.astype(BF16)
            qt[:, rows] = q.T.astype(BF16)
            gt[:, rows] = go.T.astype(BF16)

        def emit_own(jb, dk, dv):
            at = pl.ds(jb * half * kheads + h, half, stride=kheads)
            dk_ref[at, :] = dk
            dv_ref[at, :] = dv

        block("own", h, own, emit_own)

        @pl.when(h == 0)
        def _():
            relay_forward(0)

        @pl.when(h + 1 < kheads)
        def _():
            relay_forward(h + 1)

        @pl.when(has_near)
        def _():
            jax.lax.cond(
                core == 0,
                lambda: near_relay(h).wait_recv(),
                lambda: near_own(h).wait_recv(),
            )

            def emit_near(jb, dk, dv):
                gnear_out[h, jb * half:(jb + 1) * half] = dk.astype(BF16)
                gnear_out[h, tokens + jb * half:tokens + (jb + 1) * half] = dv.astype(BF16)

            block("near", h, near, emit_near)
            gnear_copy(h).start()

        @pl.when(has_far)
        def _():
            @pl.when(core == 0)
            def _():
                far_copy(h).wait_recv()

            slot = lax.rem(h, 2)

            @pl.when(jnp.logical_and(core == 1, h >= 1))
            def _():
                send_sum(h - 1)

            def emit_far(jb, dk, dv):
                held[slot, jb * half:(jb + 1) * half] = dk
                held[slot, tokens + jb * half:tokens + (jb + 1) * half] = dv

            block("far", h, far, emit_far)

            @pl.when(core == 0)
            def _():
                gfar_out[h] = held[slot].astype(BF16)
                send_back(h)

        for g in range(group):
            at = pl.ds(h * group + g, tokens, stride=qheads)
            dq_ref[at, :] = dq_acc[:, g * tokens:(g + 1) * tokens].T * SCALE

        @pl.when(h >= 2)
        def _():
            relay_back(h - 2)

        return 0

    lax.fori_loop(0, kheads, step, 0)

    @pl.when(jnp.logical_and(core == 1, has_far))
    def _():
        send_sum(kheads - 1)

    for h in range(max(kheads - 2, 0), kheads):
        relay_back(h)

    def round_query(n, _):
        rows = pl.ds(pl.multiple_of(n * tokens, tokens), tokens)
        dq_low[rows] = dq_ref[rows].astype(BF16)
        return 0

    lax.fori_loop(0, qheads, round_query, 0)
    store = pltpu.make_async_copy(dq_low, dq_hbm, store_sem)
    store.start()

    def finish(h, _):
        at = pl.ds(h, tokens, stride=kheads)

        @pl.when(core == 0)
        def _():
            gnear_copy(h).wait_recv()
            dk_ref[at, :] += gnear_in[h, 0:tokens].astype(F32)
            dv_ref[at, :] += gnear_in[h, tokens:].astype(F32)

        @pl.when(has_next)
        def _():
            gfar_copy(h).wait_recv()
            dk_ref[at, :] += gfar_in[h, 0:tokens].astype(F32)
            dv_ref[at, :] += gfar_in[h, tokens:].astype(F32)

        return 0

    lax.fori_loop(0, kheads, finish, 0)

    def round_keys(n, _):
        rows = pl.ds(pl.multiple_of(n * tokens, tokens), tokens)
        dk_out[rows] = dk_ref[rows].astype(BF16)
        dv_out[rows] = dv_ref[rows].astype(BF16)
        return 0

    lax.fori_loop(0, kheads, round_keys, 0)

    def drain(h, _):
        @pl.when(has_next)
        def _():
            far_copy(h).wait_send()

        @pl.when(gets_near)
        def _():
            near_own(h).wait_send()

        @pl.when(has_near)
        def _():
            gnear_copy(h).wait_send()

        @pl.when(has_far)
        def _():
            gfar_copy(h).wait_send()

        @pl.when(jnp.logical_or(relays_forward(h), relays_back(h)))
        def _():
            far_relay(h).wait_send()

        return 0

    lax.fori_loop(0, kheads, drain, 0)
    store.wait()


def on_device(devices, query, key, value, gradient, logsumexp, dots):
    tokens, qheads, width = query.shape
    kheads = key.shape[1]
    group = qheads // kheads
    assert WINDOW == 2 * tokens and devices % 4 == 0
    flat_q = (tokens * qheads, width)
    flat_k = (tokens * kheads, width)
    message = pltpu.VMEM((kheads, 2 * tokens, width), BF16)
    anywhere = pl.BlockSpec(memory_space=pl.ANY)
    vmem = pl.BlockSpec(memory_space=pltpu.VMEM)
    sems = pltpu.SemaphoreType.DMA((kheads,))
    dq, dk, dv = pl.pallas_call(
        functools.partial(kernel, tokens, kheads, group, devices),
        out_shape=(
            jax.ShapeDtypeStruct(flat_q, BF16),
            jax.ShapeDtypeStruct(flat_k, BF16),
            jax.ShapeDtypeStruct(flat_k, BF16),
        ),
        in_specs=[anywhere] * 4 + [vmem] * 2,
        out_specs=(anywhere, vmem, vmem),
        scratch_shapes=[
            pltpu.VMEM(flat_q, F32),
            pltpu.VMEM(flat_k, F32),
            pltpu.VMEM(flat_k, F32),
            pltpu.VMEM(flat_q, F32),
            pltpu.VMEM(flat_q, F32),
            pltpu.VMEM(flat_k, F32),
            pltpu.VMEM(flat_k, F32),
            pltpu.VMEM(flat_q, BF16),
        ] + [message] * 8 + [
            pltpu.VMEM((2, 2 * tokens, width), F32),
            pltpu.VMEM((width, group * tokens), F32),
            pltpu.VMEM((group * tokens, width), BF16),
            pltpu.VMEM((group * tokens, width), BF16),
            pltpu.VMEM((width, group * tokens), BF16),
            pltpu.VMEM((width, group * tokens), BF16),
            pltpu.SemaphoreType.DMA((4,)),
            pltpu.SemaphoreType.DMA,
        ] + [sems] * 10,
        compiler_params=pltpu.CompilerParams(
            collective_id=0, has_side_effects=True, vmem_limit_bytes=58 * 2**20
        ),
        cost_estimate=pl.CostEstimate(
            flops=10 * qheads * tokens * WINDOW * width,
            bytes_accessed=(3 * qheads + 4 * kheads) * tokens * width * 4,
            transcendentals=qheads * tokens * WINDOW,
        ),
    )(
        query.reshape(flat_q), key.reshape(flat_k), value.reshape(flat_k),
        gradient.reshape(flat_q), logsumexp, dots,
    )
    return (
        dq.astype(F32).reshape(query.shape),
        dk.astype(F32).reshape(key.shape),
        dv.astype(F32).reshape(value.shape),
    )


def solution(mesh):
    return jax.shard_map(
        functools.partial(on_device, mesh.shape["seq"]),
        mesh=mesh,
        in_specs=(
            P("seq", "head", None),
            P("seq", "head", None),
            P("seq", "head", None),
            P("seq", "head", None),
            P("head", "seq"),
            P("head", "seq"),
        ),
        out_specs=(P("seq", "head", None), P("seq", "head", None), P("seq", "head", None)),
        check_vma=False,
    )
```
